1024 devices in a mesh: section: 4 (over y), head: 8 (over x, core), tok: 32 (over z).
Axes of the slice: x: 4, y: 4, z: 32, core: 2. Of those that a mesh axis runs over, the one named last changes fastest.
Arguments:
- queries: bfloat16 [12288, 4096], P('tok', 'head'), may hold values from -10 to 10
- key_values: bfloat16 [32, 4, 96, 8, 256], P('tok', 'section', None, 'head'), may hold values from -10 to 10
- lengths: int32 [8], replicated, may hold values from 1 to 6144, 12288 in all
Outputs:
- attended: bfloat16 [12288, 4096], P('tok', 'head')
The draws below stay inside these ranges and needn't reach their ends.
All inputs are finite; a program needn't handle non-finite values.
Results may differ from the reference program's by a relative error of at most 0.0055.
Values may be sent and summed in bfloat16 or wider, within the bound.
No kernel may reach another device: no remote copies, remote signals or barrier semaphores. Data moves between devices by JAX's collectives and lax.ppermute only.
A program may use at most 32 MiB of HBM per device.

```python
import math
import jax
import jax.numpy as jnp
import numpy as np
from jax import lax

Q_HEADS = 32
KV_HEADS = 8
HEAD_DIM = 128
NDOCS = 8
TILES = 32
SPLITS = 4
KEY_ROWS = 96
TOKENS = 12288


def draw_queries(key, part):
    shape_full = (TOKENS, Q_HEADS, HEAD_DIM)
    base = jnp.clip(3.0 * jax.random.normal(jax.random.fold_in(key, 1), shape_full, jnp.float32), -9.5, 9.5)
    return base.reshape(TOKENS, Q_HEADS * HEAD_DIM).astype(jnp.bfloat16)


def draw_key_values(key, part):
    shape_full = (TOKENS, KV_HEADS, 2 * HEAD_DIM)
    base = jnp.clip(jax.random.normal(jax.random.fold_in(key, 2), shape_full, jnp.float32), -6.0, 6.0)
    return base.reshape(TILES, SPLITS, KEY_ROWS, KV_HEADS, 2 * HEAD_DIM).astype(jnp.bfloat16)


def length_profile(count, total, bound, lean):
    loads = [(1 << 20) // math.isqrt(grade ** lean) + 1 for grade in range(2, count + 1)]
    spare, given = total - bound - (count - 1), [1] * (count - 1)
    while spare > 0:
        free = [i for i in range(count - 1) if given[i] < bound]
        mass, remaining = sum([loads[i] for i in free]), spare
        for i in free:
            addition = min(bound - given[i], max(1, remaining * loads[i] // mass), spare)
            given[i] = given[i] + addition
            spare = spare - addition
    return np.array([bound] + given)


def ragged(stream_key, amount, total, most, slope):
    if amount == 2:
        one = jax.random.randint(stream_key, (), max(1, total - most), min(most, total - 1) + 1)
        return jnp.stack([one, total - one])
    sizes = jnp.asarray(length_profile(amount, total, most, slope), jnp.int32)
    couples = (amount - 1) // 2
    source_of, sink = sizes[1:1 + 2 * couples:2], sizes[2:2 + 2 * couples:2]
    slack = jnp.minimum(source_of - 1, most - sink)
    passed = jax.random.randint(jax.random.fold_in(stream_key, 1), (couples,), 0, 1 << 20) % (slack + 1)
    sizes = sizes.at[1:1 + 2 * couples:2].set(source_of - passed).at[2:2 + 2 * couples:2].set(sink + passed)
    return sizes[jax.random.permutation(jax.random.fold_in(stream_key, 2), amount)]


def setup_inputs(seed: int = 0) -> dict:
    key_of = jax.random.split(jax.random.key(seed), 4)
    return {
        "queries": draw_queries(jax.random.fold_in(key_of[3], 71), 0),
        "key_values": draw_key_values(jax.random.fold_in(key_of[3], 71), 0),
        "lengths": ragged(key_of[2], NDOCS, TOKENS, TOKENS // 2, 2).astype(jnp.int32),
    }


def doc_index(positions, ends):
    return jnp.sum((positions[:, None] >= ends[None, :]).astype(jnp.int32), axis=1)


def reference(queries, key_values, lengths):
    group = Q_HEADS // KV_HEADS
    block = math.gcd(TOKENS, 512)
    scale = HEAD_DIM ** -0.5
    table = key_values.reshape(TOKENS, KV_HEADS, 2 * HEAD_DIM)
    ends = jnp.cumsum(lengths).astype(jnp.int32)
    places = jnp.arange(TOKENS, dtype=jnp.int32)
    documents = doc_index(places, ends)

    def one_block(block_index):
        lower = (block_index * block).astype(jnp.int32)
        rows_q = lax.dynamic_slice_in_dim(queries, lower, block, 0).reshape(block, KV_HEADS, group, HEAD_DIM)
        query_pos = lower + jnp.arange(block, dtype=jnp.int32)
        query_doc = lax.dynamic_slice_in_dim(documents, lower, block, 0)
        visible = (places[None, :] <= query_pos[:, None]) & (documents[None, :] == query_doc[:, None])

        def one_group(group_index):
            heads_q = lax.dynamic_index_in_dim(rows_q, group_index, 1, keepdims=False).astype(jnp.float32)
            pair = lax.dynamic_index_in_dim(table, group_index, 1, keepdims=False)
            keys = pair[:, :HEAD_DIM].astype(jnp.float32)
            values = pair[:, HEAD_DIM:].astype(jnp.float32)
            scores = jnp.einsum("rjd,kd->jrk", heads_q, keys) * scale
            scores = jnp.where(visible[None], scores, jnp.float32(-1e30))
            peak = jnp.max(scores, axis=-1, keepdims=True)
            weights = jnp.where(visible[None], jnp.exp(scores - peak), jnp.float32(0.0))
            total = jnp.sum(weights, axis=-1)
            rounded = weights.astype(jnp.bfloat16).astype(jnp.float32)
            mixed = jnp.einsum("jrk,kd->rjd", rounded, values)
            return (mixed / jnp.transpose(total)[:, :, None]).astype(jnp.bfloat16)

        groups = lax.map(one_group, jnp.arange(KV_HEADS, dtype=jnp.int32))
        return jnp.transpose(groups, (1, 0, 2, 3)).reshape(block, Q_HEADS * HEAD_DIM)

    blocks = lax.map(one_block, jnp.arange(TOKENS // block, dtype=jnp.int32))
    return blocks.reshape(TOKENS, Q_HEADS * HEAD_DIM)
```

```python
import functools
import math

import jax
import jax.numpy as jnp
from jax import lax
from jax.experimental import pallas as pl
from jax.experimental.pallas import tpu as pltpu
from jax.sharding import PartitionSpec as P

LOW = -1e30
FLOOR = -5e29
LANES = 128
NDOCS = 8
STAT_ROWS = 32
WHOLE = pl.BlockSpec(memory_space=pltpu.VMEM)
SCALARS = pl.BlockSpec(memory_space=pltpu.SMEM)
EARLY = ((0,), (4,), (2, 6), (1, 5, 3, 7), (8,), (12,))
LATE = ((10, 14), (9, 13, 11, 15), (16,))


def shift(value, axis, by, count):
    return lax.ppermute(value, axis, [(i, (i + by) % count) for i in range(count)])


def query_bounds(info, rows):
    place = info[0] * rows + lax.broadcasted_iota(jnp.int32, (rows, LANES), 0)
    begin = jnp.zeros((rows, LANES), jnp.int32)
    end = jnp.int32(0)
    for i in range(NDOCS):
        end = end + info[2 + i]
        begin = jnp.where(end <= place, end, begin)
    return place[:, :1], begin[:, :1]


def key_places(info, rows, key_rows, distances):
    parts = []
    for d in distances:
        base = (info[0] - d) * rows + info[1] * key_rows
        parts.append(base + lax.broadcasted_iota(jnp.int32, (1, key_rows), 1))
    return jnp.concatenate(parts, axis=1)


def scores_of(query, keys):
    return lax.dot_general(
        query, keys, (((1,), (1,)), ((), ())), preferred_element_type=jnp.float32
    )


def attend(factor, query, keys, values, visible, peak, total, sums):
    scores = jnp.where(visible, scores_of(query, keys), LOW)
    top = jnp.maximum(peak, jnp.max(scores, axis=1, keepdims=True))
    weights = jnp.exp2((scores - top) * factor).astype(jnp.bfloat16)
    mixed = jnp.dot(weights, values, preferred_element_type=jnp.float32)
    decay = jnp.exp2((peak - top) * factor)
    size = sums.shape[1]
    return top, total * decay + mixed[:, size : size + 1], sums * decay + mixed[:, :size]


def gathered(refs, size):
    keys = jnp.concatenate([ref[:, :size] for ref in refs], axis=0)
    values = jnp.concatenate([ref[:, size:] for ref in refs], axis=0)
    ones = jnp.ones((values.shape[0], LANES), values.dtype)
    return keys, jnp.concatenate([values, ones], axis=1)


def pack_stats(peaks, totals, rows):
    lane = lax.broadcasted_iota(jnp.int32, (rows, LANES), 1)
    stats = jnp.zeros((rows, LANES), jnp.float32)
    count = len(peaks)
    for h in range(count):
        stats = jnp.where(lane == h, peaks[h], stats)
        stats = jnp.where(lane == 4 + h, totals[h], stats)
    return stats


def early_kernel(factor, size, key_rows, info, q_ref, *refs):
    *kv_refs, sums_ref, stats_ref = refs
    rows = q_ref.shape[0]
    heads = q_ref.shape[1] // size
    place, begin = query_bounds(info, rows)
    own_keys, own_values = gathered(kv_refs[:1], size)
    own_place = key_places(info, rows, key_rows, EARLY[0])
    own_visible = (own_place <= place) & (own_place >= begin)
    keys, values = gathered(kv_refs[1:], size)
    distances = [d for group in EARLY[1:] for d in group]
    visible = key_places(info, rows, key_rows, distances) >= begin
    peaks, totals = [], []
    for h in range(heads):
        cols = slice(h * size, (h + 1) * size)
        query = q_ref[:, cols]
        state = (
            jnp.full((rows, 1), FLOOR, jnp.float32),
            jnp.zeros((rows, 1), jnp.float32),
            jnp.zeros((rows, size), jnp.float32),
        )
        state = attend(factor, query, own_keys, own_values, own_visible, *state)
        state = attend(factor, query, keys, values, visible, *state)
        peaks.append(state[0])
        totals.append(state[1])
        sums_ref[:, cols] = state[2]
    stats_ref[...] = pack_stats(peaks, totals, rows)


def late_kernel(factor, size, key_rows, info, q_ref, sums_ref, stats_ref, *refs):
    *kv_refs, out_ref = refs
    rows = q_ref.shape[0]
    width = q_ref.shape[1]
    heads = width // size
    _, begin = query_bounds(info, rows)
    keys, values = gathered(kv_refs, size)
    distances = [d for group in LATE for d in group]
    visible = key_places(info, rows, key_rows, distances) >= begin
    peaks, totals = [], []
    for h in range(heads):
        cols = slice(h * size, (h + 1) * size)
        state = (stats_ref[:, h : h + 1], stats_ref[:, 4 + h : 5 + h], sums_ref[:, cols])
        state = attend(factor, q_ref[:, cols], keys, values, visible, *state)
        peaks.append(state[0])
        totals.append(state[1])
        out_ref[:rows, cols] = state[2].astype(jnp.bfloat16)
    stats = jnp.transpose(pack_stats(peaks, totals, rows))[:8]
    high = stats.astype(jnp.bfloat16).astype(jnp.float32)
    rest = stats - high
    middle = rest.astype(jnp.bfloat16).astype(jnp.float32)
    low = rest - middle
    packed = jnp.concatenate([high, middle, low, jnp.zeros_like(low)], axis=0)
    spare = jnp.zeros((STAT_ROWS, width - rows), jnp.float32)
    out_ref[rows:, :] = jnp.concatenate([packed, spare], axis=1).astype(jnp.bfloat16)


def merge_kernel(factor, size, *refs):
    *parts, out_ref = refs
    rows = out_ref.shape[0]
    heads = out_ref.shape[1] // size
    peaks, totals = [], []
    for part in parts:
        packed = part[rows:, :].astype(jnp.float32)[:, :rows]
        stats = packed[0:8] + packed[8:16] + packed[16:24]
        peaks.append(stats)
        totals.append(pltpu.roll(stats, 4, 0))
    top = functools.reduce(jnp.maximum, peaks)
    scaled = [jnp.exp2(jnp.minimum((peak - top) * factor, 0.0)) for peak in peaks]
    terms = [s * t for s, t in zip(scaled, totals)]
    total = (terms[0] + terms[2]) + (terms[1] + terms[3])
    shares = [s / total for s in scaled]
    blank = jnp.zeros((LANES - 8 * len(parts), rows), jnp.float32)
    shares = jnp.transpose(jnp.concatenate(shares + [blank], axis=0))
    for h in range(heads):
        cols = slice(h * size, (h + 1) * size)
        terms = [
            part[:rows, cols].astype(jnp.float32) * shares[:, 8 * i + h : 8 * i + h + 1]
            for i, part in enumerate(parts)
        ]
        out_ref[:, cols] = ((terms[0] + terms[2]) + (terms[1] + terms[3])).astype(jnp.bfloat16)


def params():
    return pltpu.CompilerParams(vmem_limit_bytes=40 * 1024 * 1024)


def cost(rows, heads, keys, size):
    pairs = rows * heads * keys
    return pl.CostEstimate(
        flops=4 * pairs * size, bytes_accessed=2 * rows * heads * size, transcendentals=pairs
    )


def early_call(factor, size, key_rows, info, queries, chunks):
    rows, width = queries.shape
    return pl.pallas_call(
        functools.partial(early_kernel, factor, size, key_rows),
        out_shape=(
            jax.ShapeDtypeStruct((rows, width), jnp.float32),
            jax.ShapeDtypeStruct((rows, LANES), jnp.float32),
        ),
        in_specs=[SCALARS] + [WHOLE] * (1 + len(chunks)),
        out_specs=(WHOLE, WHOLE),
        compiler_params=params(),
        cost_estimate=cost(rows, width // size, 10 * key_rows, size),
        name="early",
    )(info, queries, *chunks)


def late_call(factor, size, key_rows, info, queries, state, chunks):
    rows, width = queries.shape
    return pl.pallas_call(
        functools.partial(late_kernel, factor, size, key_rows),
        out_shape=jax.ShapeDtypeStruct((rows + STAT_ROWS, width), jnp.bfloat16),
        in_specs=[SCALARS] + [WHOLE] * (3 + len(chunks)),
        out_specs=WHOLE,
        compiler_params=params(),
        cost_estimate=cost(rows, width // size, 7 * key_rows, size),
        name="late",
    )(info, queries, *state, *chunks)


def merge_call(factor, size, rows, parts):
    width = parts[0].shape[1]
    return pl.pallas_call(
        functools.partial(merge_kernel, factor, size),
        out_shape=jax.ShapeDtypeStruct((rows, width), jnp.bfloat16),
        in_specs=[WHOLE] * len(parts),
        out_specs=WHOLE,
        compiler_params=params(),
        name="merge",
    )(*parts)


def shards(tiles, splits, queries, key_values, lengths):
    rows = queries.shape[0]
    key_rows = key_values.shape[2]
    size = key_values.shape[4] // 2
    factor = size ** (-0.5) * math.log2(math.e)
    place = jnp.stack([lax.axis_index("tok"), lax.axis_index("section")]).astype(jnp.int32)
    info = jnp.concatenate([place, lengths])
    own = key_values.reshape(key_rows, 2 * size)
    along = lambda value, by: shift(value, "tok", by, tiles)
    far = along(own, 8)
    near4 = along(own, 4)
    near2 = along(jnp.concatenate([own, near4]), 2)
    far4 = along(far, 4)
    near1 = along(jnp.concatenate([own, near4, near2]), 1)
    far2 = along(jnp.concatenate([far, far4]), 2)
    far1 = along(jnp.concatenate([far, far4, far2]), 1)
    last = along(far2[key_rows:], 2)
    state = early_call(
        factor, size, key_rows, info, queries, (own, near4, near2, near1, far, far4)
    )
    part = late_call(factor, size, key_rows, info, queries, state, (far2, far1, last))
    parts = [part] + [shift(part, "section", by, splits) for by in range(1, splits)]
    return merge_call(factor, size, rows, parts)


def solution(mesh):
    return jax.shard_map(
        functools.partial(shards, mesh.shape["tok"], mesh.shape["section"]),
        mesh=mesh,
        in_specs=(P("tok", "head"), P("tok", "section", None, "head", None), P()),
        out_specs=P("tok", "head"),
        check_vma=False,
    )
```

```python
import functools
import math

import jax
import jax.numpy as jnp
from jax import lax
from jax.experimental import pallas as pl
from jax.experimental.pallas import tpu as pltpu
from jax.sharding import PartitionSpec as P

LOW = -1e30
FLOOR = -5e29
LANES = 128
NDOCS = 8
STAT_ROWS = 16
WHOLE = pl.BlockSpec(memory_space=pltpu.VMEM)
SCALARS = pl.BlockSpec(memory_space=pltpu.SMEM)
PLAN = (
    (6, (0,)),
    (6, (6,)),
    (3, (0, 6, 12)),
    (1, (0, 6, 12, 3, 9, 15)),
    (-1, (6, 12, 3, 9, 15)),
)
STAGES = ((-1, 0, 1, 2), (3,), (4,))


def distances_of(arrival):
    by, carried = PLAN[arrival]
    return (0,) if arrival < 0 else tuple(d + by for d in carried)


def shift(value, axis, by, count):
    return lax.ppermute(value, axis, [(i, (i + by) % count) for i in range(count)])


def joined(pieces, key_rows):
    runs = []
    for array, row in pieces:
        if runs and runs[-1][0] is array and runs[-1][2] == row:
            runs[-1][2] = row + key_rows
        else:
            runs.append([array, row, row + key_rows])
    cuts = [array if hi - lo == array.shape[0] else array[lo:hi] for array, lo, hi in runs]
    return jnp.concatenate(cuts) if len(cuts) > 1 else cuts[0]


def query_bounds(lengths, rows):
    place = lax.axis_index("tok") * rows + lax.broadcasted_iota(jnp.int32, (rows, LANES), 0)
    begin = jnp.zeros((rows, LANES), jnp.int32)
    end = jnp.int32(0)
    for i in range(NDOCS):
        end = end + lengths[i]
        begin = jnp.where(end <= place, end, begin)
    return place[:, :1], begin[:, :1]


def key_places(rows, key_rows, distances):
    tile, split = lax.axis_index("tok"), lax.axis_index("section")
    parts = []
    for d in distances:
        base = (tile - d) * rows + split * key_rows
        parts.append(base + lax.broadcasted_iota(jnp.int32, (1, key_rows), 1))
    return jnp.concatenate(parts, axis=1)


def scores_of(query, keys):
    return lax.dot_general(
        query, keys, (((1,), (1,)), ((), ())), preferred_element_type=jnp.float32
    )


def attend(factor, query, keys, values, visible, peak, total, sums):
    scores = jnp.where(visible, scores_of(query, keys), LOW)
    top = jnp.maximum(peak, jnp.max(scores, axis=1, keepdims=True))
    weights = jnp.exp2((scores - top) * factor).astype(jnp.bfloat16)
    mixed = jnp.dot(weights, values, preferred_element_type=jnp.float32)
    decay = jnp.exp2((peak - top) * factor)
    size = sums.shape[1]
    return top, total * decay + mixed[:, size : size + 1], sums * decay + mixed[:, :size]


def gathered(refs, size):
    keys = jnp.concatenate([ref[:, :size] for ref in refs], axis=0)
    values = jnp.concatenate([ref[:, size:] for ref in refs], axis=0)
    ones = jnp.ones((values.shape[0], LANES), values.dtype)
    return keys, jnp.concatenate([values, ones], axis=1)


def stage_kernel(factor, size, key_rows, stage, lengths, q_ref, *refs):
    first, last = stage == 0, stage == len(STAGES) - 1
    arrivals = STAGES[stage]
    rows, width = q_ref.shape
    heads = width // size
    place, begin = query_bounds(lengths, rows)
    if not first:
        sums_in, stats_in, *refs = refs
    if last:
        *kv_refs, out_ref = refs
    else:
        *kv_refs, sums_out, stats_out = refs
    if first:
        own_keys, own_values = gathered(kv_refs[:1], size)
        own_place = key_places(rows, key_rows, (0,))
        own_visible = (own_place <= place) & (own_place >= begin)
        arrivals, kv_refs = arrivals[1:], kv_refs[1:]
    keys, values = gathered(kv_refs, size)
    distances = [d for arrival in arrivals for d in distances_of(arrival)]
    visible = key_places(rows, key_rows, distances) >= begin
    lane = lax.broadcasted_iota(jnp.int32, (rows, LANES), 1)
    stats = jnp.full((rows, LANES), LOW, jnp.float32)
    for h in range(heads):
        cols = slice(h * size, (h + 1) * size)
        query = q_ref[:, cols]
        if first:
            state = (
                jnp.full((rows, 1), FLOOR, jnp.float32),
                jnp.zeros((rows, 1), jnp.float32),
                jnp.zeros((rows, size), jnp.float32),
            )
            state = attend(factor, query, own_keys, own_values, own_visible, *state)
        else:
            state = (stats_in[:, h : h + 1], stats_in[:, 4 + h : 5 + h], sums_in[:, cols])
        peak, total, sums = attend(factor, query, keys, values, visible, *state)
        if not last:
            stats = jnp.where(lane == h, peak, stats)
            stats = jnp.where(lane == 4 + h, total, stats)
            sums_out[:, cols] = sums
            continue
        some = total > 0.0
        level = jnp.where(some, peak * factor + jnp.log2(jnp.where(some, total, 1.0)), LOW)
        stats = jnp.where(lane == h, level, stats)
        share = jnp.where(some, 1.0 / jnp.where(some, total, 1.0), 0.0)
        out_ref[:rows, cols] = (sums * share).astype(jnp.bfloat16)
    if not last:
        stats_out[...] = stats
        return
    levels = jnp.transpose(stats)[:8]
    high = levels.astype(jnp.bfloat16).astype(jnp.float32)
    rest = levels - high
    middle = rest.astype(jnp.bfloat16).astype(jnp.float32)
    low = rest - middle
    row = lax.broadcasted_iota(jnp.int32, high.shape, 0)
    packed = jnp.concatenate([jnp.where(row < 4, high, pltpu.roll(middle, 4, 0)), low], axis=0)
    spare = jnp.zeros((STAT_ROWS, width - rows), jnp.float32)
    out_ref[rows:, :] = jnp.concatenate([packed, spare], axis=1).astype(jnp.bfloat16)


def merge_kernel(size, *refs):
    *parts, out_ref = refs
    rows = out_ref.shape[0]
    heads = out_ref.shape[1] // size
    levels = []
    for part in parts:
        packed = part[rows:, :].astype(jnp.float32)[:, :rows]
        levels.append((packed[:8] + pltpu.roll(packed[:8], 4, 0)) + packed[8:])
    top = functools.reduce(jnp.maximum, levels)
    terms = [jnp.exp2(level - top) for level in levels]
    total = (terms[0] + terms[2]) + (terms[1] + terms[3])
    shares = [term / total for term in terms]
    blank = jnp.zeros((LANES - 8 * len(parts), rows), jnp.float32)
    shares = jnp.transpose(jnp.concatenate(shares + [blank], axis=0))
    for h in range(heads):
        cols = slice(h * size, (h + 1) * size)
        terms = [
            part[:rows, cols].astype(jnp.float32) * shares[:, 8 * i + h : 8 * i + h + 1]
            for i, part in enumerate(parts)
        ]
        out_ref[:, cols] = ((terms[0] + terms[2]) + (terms[1] + terms[3])).astype(jnp.bfloat16)


def params():
    return pltpu.CompilerParams(vmem_limit_bytes=40 * 1024 * 1024)


def cost(rows, heads, keys, size):
    pairs = rows * heads * keys
    return pl.CostEstimate(
        flops=4 * pairs * size, bytes_accessed=2 * rows * heads * size, transcendentals=pairs
    )


def stage_call(factor, size, key_rows, stage, lengths, queries, state, chunks):
    rows, width = queries.shape
    keys = sum(len(distances_of(arrival)) for arrival in STAGES[stage]) * key_rows
    if stage == len(STAGES) - 1:
        out_shape = jax.ShapeDtypeStruct((rows + STAT_ROWS, width), jnp.bfloat16)
        out_specs = WHOLE
    else:
        out_shape = (
            jax.ShapeDtypeStruct((rows, width), jnp.float32),
            jax.ShapeDtypeStruct((rows, LANES), jnp.float32),
        )
        out_specs = (WHOLE, WHOLE)
    return pl.pallas_call(
        functools.partial(stage_kernel, factor, size, key_rows, stage),
        out_shape=out_shape,
        in_specs=[SCALARS] + [WHOLE] * (1 + len(state) + len(chunks)),
        out_specs=out_specs,
        compiler_params=params(),
        cost_estimate=cost(rows, width // size, keys, size),
        name="attend" + str(stage),
    )(lengths, queries, *state, *chunks)


def merge_call(size, rows, parts):
    width = parts[0].shape[1]
    return pl.pallas_call(
        functools.partial(merge_kernel, size),
        out_shape=jax.ShapeDtypeStruct((rows, width), jnp.bfloat16),
        in_specs=[WHOLE] * len(parts),
        out_specs=WHOLE,
        compiler_params=params(),
        name="merge",
    )(*parts)


def shards(tiles, splits, queries, key_values, lengths):
    rows = queries.shape[0]
    key_rows = key_values.shape[2]
    size = key_values.shape[4] // 2
    factor = size ** (-0.5) * math.log2(math.e)
    own = key_values.reshape(key_rows, 2 * size)
    held = {0: (own, 0)}
    arrived = []
    for by, carried in PLAN:
        cargo = joined([held[d] for d in carried], key_rows)
        result = shift(cargo, "tok", by, tiles)
        arrived.append(result)
        for i, d in enumerate(carried):
            held[d] = (cargo, i * key_rows)
            held[d + by] = (result, i * key_rows)
    state = ()
    for stage, arrivals in enumerate(STAGES):
        chunks = [own if arrival < 0 else arrived[arrival] for arrival in arrivals]
        state = stage_call(factor, size, key_rows, stage, lengths, queries, state, chunks)
    part = state
    parts = [part] + [shift(part, "section", by, splits) for by in range(1, splits)]
    return merge_call(size, rows, parts)


def solution(mesh):
    return jax.shard_map(
        functools.partial(shards, mesh.shape["tok"], mesh.shape["section"]),
        mesh=mesh,
        in_specs=(P("tok", "head"), P("tok", "section", None, "head", None), P()),
        out_specs=P("tok", "head"),
        check_vma=False,
    )
```

```python
import functools
import math

import jax
import jax.numpy as jnp
from jax import lax
from jax.experimental import pallas as pl
from jax.experimental.pallas import tpu as pltpu
from jax.sharding import PartitionSpec as P

LOW = -1e30
FLOOR = -5e29
LANES = 128
NDOCS = 8
STAT_ROWS = 16
WHOLE = pl.BlockSpec(memory_space=pltpu.VMEM)
SCALARS = pl.BlockSpec(memory_space=pltpu.SMEM)
PLAN = (
    (6, (0,)),
    (6, (6,)),
    (3, (0, 6, 12)),
    (1, (0, 6, 12, 3, 9, 15)),
    (-1, (6, 12, 3, 9, 15)),
)
STAGES = ((-1, 0, 1, 2), (3,), (4,))


def distances_of(arrival):
    by, carried = PLAN[arrival]
    return (0,) if arrival < 0 else tuple(d + by for d in carried)


def shift(value, axis, by, count):
    return lax.ppermute(value, axis, [(i, (i + by) % count) for i in range(count)])


def joined(pieces, key_rows):
    runs = []
    for array, row in pieces:
        if runs and runs[-1][0] is array and runs[-1][2] == row:
            runs[-1][2] = row + key_rows
        else:
            runs.append([array, row, row + key_rows])
    cuts = [array if hi - lo == array.shape[0] else array[lo:hi] for array, lo, hi in runs]
    return jnp.concatenate(cuts) if len(cuts) > 1 else cuts[0]


def query_bounds(lengths, rows):
    place = lax.axis_index("tok") * rows + lax.broadcasted_iota(jnp.int32, (rows, LANES), 0)
    begin = jnp.zeros((rows, LANES), jnp.int32)
    end = jnp.int32(0)
    for i in range(NDOCS):
        end = end + lengths[i]
        begin = jnp.where(end <= place, end, begin)
    return begin


def bounds_kernel(lengths, begin_ref):
    begin_ref[...] = query_bounds(lengths, begin_ref.shape[0])


def bounds_call(lengths, rows):
    return pl.pallas_call(
        bounds_kernel,
        out_shape=jax.ShapeDtypeStruct((rows, LANES), jnp.int32),
        in_specs=[SCALARS],
        out_specs=WHOLE,
        compiler_params=params(),
        name="bounds",
    )(lengths)


def key_places(rows, key_rows, distances):
    tile, split = lax.axis_index("tok"), lax.axis_index("section")
    parts = []
    for d in distances:
        base = (tile - d) * rows + split * key_rows
        parts.append(base + lax.broadcasted_iota(jnp.int32, (1, key_rows), 1))
    return jnp.concatenate(parts, axis=1)


def scores_of(query, keys):
    return lax.dot_general(
        query, keys, (((1,), (1,)), ((), ())), preferred_element_type=jnp.float32
    )


def attend(factor, query, keys, values, visible, peak, total, sums):
    scores = jnp.where(visible, scores_of(query, keys), LOW)
    top = jnp.maximum(peak, jnp.max(scores, axis=1, keepdims=True))
    weights = jnp.exp2((scores - top) * factor).astype(jnp.bfloat16)
    mixed = jnp.dot(weights, values, preferred_element_type=jnp.float32)
    decay = jnp.exp2((peak - top) * factor)
    size = sums.shape[1]
    return top, total * decay + mixed[:, size:], sums * decay + mixed[:, :size]


def gathered(refs, size):
    keys = jnp.concatenate([ref[:, :size] for ref in refs], axis=0)
    values = jnp.concatenate([ref[:, size:] for ref in refs], axis=0)
    ones = jnp.ones((values.shape[0], LANES), values.dtype)
    return keys, jnp.concatenate([values, ones], axis=1)


def stage_kernel(factor, size, key_rows, stage, begin_ref, q_ref, *refs):
    first, last = stage == 0, stage == len(STAGES) - 1
    arrivals = STAGES[stage]
    rows, width = q_ref.shape
    heads = width // size
    begin = begin_ref[:, :1]
    if not first:
        sums_in, totals_in, stats_in, *refs = refs
    if last:
        *kv_refs, out_ref = refs
    else:
        *kv_refs, sums_out, totals_out, stats_out = refs
    if first:
        place = lax.axis_index("tok") * rows + lax.broadcasted_iota(jnp.int32, (rows, 1), 0)
        own_keys, own_values = gathered(kv_refs[:1], size)
        own_place = key_places(rows, key_rows, (0,))
        own_visible = (own_place <= place) & (own_place >= begin)
        arrivals, kv_refs = arrivals[1:], kv_refs[1:]
    keys, values = gathered(kv_refs, size)
    distances = [d for arrival in arrivals for d in distances_of(arrival)]
    visible = key_places(rows, key_rows, distances) >= begin
    lane = lax.broadcasted_iota(jnp.int32, (rows, LANES), 1)
    stats = jnp.full((rows, LANES), LOW, jnp.float32)
    packed = jnp.ones((rows, LANES), jnp.float32)
    for h in range(heads):
        cols = slice(h * size, (h + 1) * size)
        query = q_ref[:, cols]
        if first:
            state = (
                jnp.full((rows, 1), FLOOR, jnp.float32),
                jnp.zeros((rows, LANES), jnp.float32),
                jnp.zeros((rows, size), jnp.float32),
            )
            state = attend(factor, query, own_keys, own_values, own_visible, *state)
        else:
            state = (stats_in[:, h : h + 1], totals_in[:, cols], sums_in[:, cols])
        peak, total, sums = attend(factor, query, keys, values, visible, *state)
        if not last:
            stats = jnp.where(lane == h, peak, stats)
            totals_out[:, cols] = total
            sums_out[:, cols] = sums
            continue
        stats = jnp.where(lane == h, peak, stats)
        packed = jnp.where(lane == h, total, packed)
        out_ref[:rows, cols] = (sums / jnp.maximum(total, 1e-30)).astype(jnp.bfloat16)
    if not last:
        stats_out[...] = stats
        return
    stats = stats * factor + jnp.log2(jnp.maximum(packed, 1e-30))
    stats = jnp.where(packed > 0.0, stats, LOW)
    levels = jnp.transpose(stats)[:8]
    high = levels.astype(jnp.bfloat16).astype(jnp.float32)
    rest = levels - high
    middle = rest.astype(jnp.bfloat16).astype(jnp.float32)
    low = rest - middle
    row = lax.broadcasted_iota(jnp.int32, high.shape, 0)
    packed = jnp.concatenate([jnp.where(row < 4, high, pltpu.roll(middle, 4, 0)), low], axis=0)
    spare = jnp.zeros((STAT_ROWS, width - rows), jnp.float32)
    out_ref[rows:, :] = jnp.concatenate([packed, spare], axis=1).astype(jnp.bfloat16)


def merge_kernel(size, *refs):
    *parts, out_ref = refs
    rows = out_ref.shape[0]
    heads = out_ref.shape[1] // size
    levels = []
    for part in parts:
        packed = part[rows:, :].astype(jnp.float32)[:, :rows]
        levels.append((packed[:8] + pltpu.roll(packed[:8], 4, 0)) + packed[8:])
    top = functools.reduce(jnp.maximum, levels)
    terms = [jnp.exp2(level - top) for level in levels]
    total = (terms[0] + terms[2]) + (terms[1] + terms[3])
    shares = [term / total for term in terms]
    blank = jnp.zeros((LANES - 8 * len(parts), rows), jnp.float32)
    shares = jnp.transpose(jnp.concatenate(shares + [blank], axis=0))
    for h in range(heads):
        cols = slice(h * size, (h + 1) * size)
        terms = [
            part[:rows, cols].astype(jnp.float32) * shares[:, 8 * i + h : 8 * i + h + 1]
            for i, part in enumerate(parts)
        ]
        out_ref[:, cols] = ((terms[0] + terms[2]) + (terms[1] + terms[3])).astype(jnp.bfloat16)


def params():
    return pltpu.CompilerParams(vmem_limit_bytes=40 * 1024 * 1024)


def cost(rows, heads, keys, size):
    pairs = rows * heads * keys
    return pl.CostEstimate(
        flops=4 * pairs * size, bytes_accessed=2 * rows * heads * size, transcendentals=pairs
    )


def stage_call(factor, size, key_rows, stage, begin, queries, state, chunks):
    rows, width = queries.shape
    keys = sum(len(distances_of(arrival)) for arrival in STAGES[stage]) * key_rows
    if stage == len(STAGES) - 1:
        out_shape = jax.ShapeDtypeStruct((rows + STAT_ROWS, width), jnp.bfloat16)
        out_specs = WHOLE
    else:
        out_shape = (
            jax.ShapeDtypeStruct((rows, width), jnp.float32),
            jax.ShapeDtypeStruct((rows, width), jnp.float32),
            jax.ShapeDtypeStruct((rows, LANES), jnp.float32),
        )
        out_specs = (WHOLE, WHOLE, WHOLE)
    return pl.pallas_call(
        functools.partial(stage_kernel, factor, size, key_rows, stage),
        out_shape=out_shape,
        in_specs=[WHOLE] * (2 + len(state) + len(chunks)),
        out_specs=out_specs,
        compiler_params=params(),
        cost_estimate=cost(rows, width // size, keys, size),
        name="attend" + str(stage),
    )(begin, queries, *state, *chunks)


def merge_call(size, rows, parts):
    width = parts[0].shape[1]
    return pl.pallas_call(
        functools.partial(merge_kernel, size),
        out_shape=jax.ShapeDtypeStruct((rows, width), jnp.bfloat16),
        in_specs=[WHOLE] * len(parts),
        out_specs=WHOLE,
        compiler_params=params(),
        name="merge",
    )(*parts)


def shards(tiles, splits, queries, key_values, lengths):
    rows = queries.shape[0]
    key_rows = key_values.shape[2]
    size = key_values.shape[4] // 2
    factor = size ** (-0.5) * math.log2(math.e)
    own = key_values.reshape(key_rows, 2 * size)
    held = {0: (own, 0)}
    arrived = []
    for by, carried in PLAN:
        cargo = joined([held[d] for d in carried], key_rows)
        result = shift(cargo, "tok", by, tiles)
        arrived.append(result)
        for i, d in enumerate(carried):
            held[d] = (cargo, i * key_rows)
            held[d + by] = (result, i * key_rows)
    begin = bounds_call(lengths, rows)
    state = ()
    for stage, arrivals in enumerate(STAGES):
        chunks = [own if arrival < 0 else arrived[arrival] for arrival in arrivals]
        state = stage_call(factor, size, key_rows, stage, begin, queries, state, chunks)
    part = state
    parts = [part] + [shift(part, "section", by, splits) for by in range(1, splits)]
    return merge_call(size, rows, parts)


def solution(mesh):
    return jax.shard_map(
        functools.partial(shards, mesh.shape["tok"], mesh.shape["section"]),
        mesh=mesh,
        in_specs=(P("tok", "head"), P("tok", "section", None, "head", None), P()),
        out_specs=P("tok", "head"),
        check_vma=False,
    )
```

```python
import functools
import math

import jax
import jax.numpy as jnp
from jax import lax
from jax.experimental import pallas as pl
from jax.experimental.pallas import tpu as pltpu
from jax.sharding import PartitionSpec as P

LOW = -1e30
FLOOR = -5e29
LANES = 128
NDOCS = 8
STAT_ROWS = 16
WHOLE = pl.BlockSpec(memory_space=pltpu.VMEM)
SCALARS = pl.BlockSpec(memory_space=pltpu.SMEM)
PLAN = (
    (6, (0,)),
    (6, (6,)),
    (3, (0, 6, 12)),
    (1, (0, 6, 12, 3, 9, 15)),
    (-1, (6, 12, 3, 9, 15)),
)
STAGES = ((-1, 0, 1), (2, 3), (4,))


def distances_of(arrival):
    by, carried = PLAN[arrival]
    return (0,) if arrival < 0 else tuple(d + by for d in carried)


def shift(value, axis, by, count):
    return lax.ppermute(value, axis, [(i, (i + by) % count) for i in range(count)])


def joined(pieces, key_rows):
    runs = []
    for array, row in pieces:
        if runs and runs[-1][0] is array and runs[-1][2] == row:
            runs[-1][2] = row + key_rows
        else:
            runs.append([array, row, row + key_rows])
    cuts = [array if hi - lo == array.shape[0] else array[lo:hi] for array, lo, hi in runs]
    return jnp.concatenate(cuts) if len(cuts) > 1 else cuts[0]


def query_bounds(lengths, rows):
    place = lax.axis_index("tok") * rows + lax.broadcasted_iota(jnp.int32, (rows, LANES), 0)
    begin = jnp.zeros((rows, LANES), jnp.int32)
    end = jnp.int32(0)
    for i in range(NDOCS):
        end = end + lengths[i]
        begin = jnp.where(end <= place, end, begin)
    return begin


def bounds_kernel(lengths, begin_ref):
    begin_ref[...] = query_bounds(lengths, begin_ref.shape[0])


def bounds_call(lengths, rows):
    return pl.pallas_call(
        bounds_kernel,
        out_shape=jax.ShapeDtypeStruct((rows, LANES), jnp.int32),
        in_specs=[SCALARS],
        out_specs=WHOLE,
        compiler_params=params(),
        name="bounds",
    )(lengths)


def key_places(rows, key_rows, distances):
    tile, split = lax.axis_index("tok"), lax.axis_index("section")
    parts = []
    for d in distances:
        base = (tile - d) * rows + split * key_rows
        parts.append(base + lax.broadcasted_iota(jnp.int32, (1, key_rows), 1))
    return jnp.concatenate(parts, axis=1)


def scores_of(query, keys):
    return lax.dot_general(
        query, keys, (((1,), (1,)), ((), ())), preferred_element_type=jnp.float32
    )


def attend(factor, query, keys, values, visible, peak, total, sums):
    scores = jnp.where(visible, scores_of(query, keys), LOW)
    top = jnp.maximum(peak, jnp.max(scores, axis=1, keepdims=True))
    weights = jnp.exp2((scores - top) * factor).astype(jnp.bfloat16)
    mixed = jnp.dot(weights, values, preferred_element_type=jnp.float32)
    decay = jnp.exp2((peak - top) * factor)
    size = sums.shape[1]
    return top, total * decay + mixed[:, size:], sums * decay + mixed[:, :size]


def gathered(refs, size):
    keys = jnp.concatenate([ref[:, :size] for ref in refs], axis=0)
    values = jnp.concatenate([ref[:, size:] for ref in refs], axis=0)
    ones = jnp.ones((values.shape[0], LANES), values.dtype)
    return keys, jnp.concatenate([values, ones], axis=1)


def stage_kernel(factor, size, key_rows, stage, begin_ref, q_ref, *refs):
    first, last = stage == 0, stage == len(STAGES) - 1
    arrivals = STAGES[stage]
    rows, width = q_ref.shape
    heads = width // size
    begin = begin_ref[:, :1]
    if not first:
        sums_in, totals_in, stats_in, *refs = refs
    if last:
        *kv_refs, out_ref = refs
    else:
        *kv_refs, sums_out, totals_out, stats_out = refs
    if first:
        place = lax.axis_index("tok") * rows + lax.broadcasted_iota(jnp.int32, (rows, 1), 0)
        own_keys, own_values = gathered(kv_refs[:1], size)
        own_place = key_places(rows, key_rows, (0,))
        own_visible = (own_place <= place) & (own_place >= begin)
        arrivals, kv_refs = arrivals[1:], kv_refs[1:]
    keys, values = gathered(kv_refs, size)
    distances = [d for arrival in arrivals for d in distances_of(arrival)]
    visible = key_places(rows, key_rows, distances) >= begin
    lane = lax.broadcasted_iota(jnp.int32, (rows, LANES), 1)
    stats = jnp.full((rows, LANES), LOW, jnp.float32)
    packed = jnp.ones((rows, LANES), jnp.float32)
    for h in range(heads):
        cols = slice(h * size, (h + 1) * size)
        query = q_ref[:, cols]
        if first:
            state = (
                jnp.full((rows, 1), FLOOR, jnp.float32),
                jnp.zeros((rows, LANES), jnp.float32),
                jnp.zeros((rows, size), jnp.float32),
            )
            state = attend(factor, query, own_keys, own_values, own_visible, *state)
        else:
            state = (stats_in[:, h : h + 1], totals_in[:, cols], sums_in[:, cols])
        peak, total, sums = attend(factor, query, keys, values, visible, *state)
        if not last:
            stats = jnp.where(lane == h, peak, stats)
            totals_out[:, cols] = total
            sums_out[:, cols] = sums
            continue
        stats = jnp.where(lane == h, peak, stats)
        packed = jnp.where(lane == h, total, packed)
        out_ref[:rows, cols] = (sums / jnp.maximum(total, 1e-30)).astype(jnp.bfloat16)
    if not last:
        stats_out[...] = stats
        return
    stats = stats * factor + jnp.log2(jnp.maximum(packed, 1e-30))
    stats = jnp.where(packed > 0.0, stats, LOW)
    levels = jnp.transpose(stats)[:8]
    high = levels.astype(jnp.bfloat16).astype(jnp.float32)
    rest = levels - high
    middle = rest.astype(jnp.bfloat16).astype(jnp.float32)
    low = rest - middle
    row = lax.broadcasted_iota(jnp.int32, high.shape, 0)
    packed = jnp.concatenate([jnp.where(row < 4, high, pltpu.roll(middle, 4, 0)), low], axis=0)
    spare = jnp.zeros((STAT_ROWS, width - rows), jnp.float32)
    out_ref[rows:, :] = jnp.concatenate([packed, spare], axis=1).astype(jnp.bfloat16)


def merge_kernel(size, *refs):
    *parts, out_ref = refs
    rows = out_ref.shape[0]
    heads = out_ref.shape[1] // size
    levels = []
    for part in parts:
        packed = part[rows:, :].astype(jnp.float32)[:, :rows]
        levels.append((packed[:8] + pltpu.roll(packed[:8], 4, 0)) + packed[8:])
    top = functools.reduce(jnp.maximum, levels)
    terms = [jnp.exp2(level - top) for level in levels]
    total = (terms[0] + terms[2]) + (terms[1] + terms[3])
    shares = [term / total for term in terms]
    blank = jnp.zeros((LANES - 8 * len(parts), rows), jnp.float32)
    shares = jnp.transpose(jnp.concatenate(shares + [blank], axis=0))
    for h in range(heads):
        cols = slice(h * size, (h + 1) * size)
        terms = [
            part[:rows, cols].astype(jnp.float32) * shares[:, 8 * i + h : 8 * i + h + 1]
            for i, part in enumerate(parts)
        ]
        out_ref[:, cols] = ((terms[0] + terms[2]) + (terms[1] + terms[3])).astype(jnp.bfloat16)


def params():
    return pltpu.CompilerParams(vmem_limit_bytes=40 * 1024 * 1024)


def cost(rows, heads, keys, size):
    pairs = rows * heads * keys
    return pl.CostEstimate(
        flops=4 * pairs * size, bytes_accessed=2 * rows * heads * size, transcendentals=pairs
    )


def stage_call(factor, size, key_rows, stage, begin, queries, state, chunks):
    rows, width = queries.shape
    keys = sum(len(distances_of(arrival)) for arrival in STAGES[stage]) * key_rows
    if stage == len(STAGES) - 1:
        out_shape = jax.ShapeDtypeStruct((rows + STAT_ROWS, width), jnp.bfloat16)
        out_specs = WHOLE
    else:
        out_shape = (
            jax.ShapeDtypeStruct((rows, width), jnp.float32),
            jax.ShapeDtypeStruct((rows, width), jnp.float32),
            jax.ShapeDtypeStruct((rows, LANES), jnp.float32),
        )
        out_specs = (WHOLE, WHOLE, WHOLE)
    return pl.pallas_call(
        functools.partial(stage_kernel, factor, size, key_rows, stage),
        out_shape=out_shape,
        in_specs=[WHOLE] * (2 + len(state) + len(chunks)),
        out_specs=out_specs,
        compiler_params=params(),
        cost_estimate=cost(rows, width // size, keys, size),
        name="attend" + str(stage),
    )(begin, queries, *state, *chunks)


def merge_call(size, rows, parts):
    width = parts[0].shape[1]
    return pl.pallas_call(
        functools.partial(merge_kernel, size),
        out_shape=jax.ShapeDtypeStruct((rows, width), jnp.bfloat16),
        in_specs=[WHOLE] * len(parts),
        out_specs=WHOLE,
        compiler_params=params(),
        name="merge",
    )(*parts)


def shards(tiles, splits, queries, key_values, lengths):
    rows = queries.shape[0]
    key_rows = key_values.shape[2]
    size = key_values.shape[4] // 2
    factor = size ** (-0.5) * math.log2(math.e)
    own = key_values.reshape(key_rows, 2 * size)
    held = {0: (own, 0)}
    arrived = []
    for by, carried in PLAN:
        cargo = joined([held[d] for d in carried], key_rows)
        result = shift(cargo, "tok", by, tiles)
        arrived.append(result)
        for i, d in enumerate(carried):
            held[d] = (cargo, i * key_rows)
            held[d + by] = (result, i * key_rows)
    begin = bounds_call(lengths, rows)
    state = ()
    for stage, arrivals in enumerate(STAGES):
        chunks = [own if arrival < 0 else arrived[arrival] for arrival in arrivals]
        state = stage_call(factor, size, key_rows, stage, begin, queries, state, chunks)
    part = state
    parts = [part] + [shift(part, "section", by, splits) for by in range(1, splits)]
    return merge_call(size, rows, parts)


def solution(mesh):
    return jax.shard_map(
        functools.partial(shards, mesh.shape["tok"], mesh.shape["section"]),
        mesh=mesh,
        in_specs=(P("tok", "head"), P("tok", "section", None, "head", None), P()),
        out_specs=P("tok", "head"),
        check_vma=False,
    )
```

```python
import functools
import math

import jax
import jax.numpy as jnp
from jax import lax
from jax.experimental import pallas as pl
from jax.experimental.pallas import tpu as pltpu
from jax.sharding import PartitionSpec as P

LOW = -1e30
FLOOR = -5e29
LANES = 128
NDOCS = 8
STAT_ROWS = 16
WHOLE = pl.BlockSpec(memory_space=pltpu.VMEM)
SCALARS = pl.BlockSpec(memory_space=pltpu.SMEM)
PLAN = (
    (6, (0,)),
    (6, (6,)),
    (3, (0, 6, 12)),
    (1, (0, 6, 12, 3, 9, 15)),
    (-1, (6, 12, 3, 9, 15)),
)
STAGES = ((-1, 0, 1), (2, 3), (4,))
AHEAD = 3


def distances_of(arrival):
    by, carried = PLAN[arrival]
    return (0,) if arrival < 0 else tuple(d + by for d in carried)


def shift(value, axis, by, count):
    return lax.ppermute(value, axis, [(i, (i + by) % count) for i in range(count)])


def joined(pieces, key_rows):
    runs = []
    for array, row in pieces:
        if runs and runs[-1][0] is array and runs[-1][2] == row:
            runs[-1][2] = row + key_rows
        else:
            runs.append([array, row, row + key_rows])
    cuts = [array if hi - lo == array.shape[0] else array[lo:hi] for array, lo, hi in runs]
    return jnp.concatenate(cuts) if len(cuts) > 1 else cuts[0]


def query_bounds(lengths, rows):
    place = lax.axis_index("tok") * rows + lax.broadcasted_iota(jnp.int32, (rows, LANES), 0)
    begin = jnp.zeros((rows, LANES), jnp.int32)
    end = jnp.int32(0)
    for i in range(NDOCS):
        end = end + lengths[i]
        begin = jnp.where(end <= place, end, begin)
    return begin


def bounds_kernel(lengths, begin_ref):
    begin_ref[...] = query_bounds(lengths, begin_ref.shape[0])


def bounds_call(lengths, rows):
    return pl.pallas_call(
        bounds_kernel,
        out_shape=jax.ShapeDtypeStruct((rows, LANES), jnp.int32),
        in_specs=[SCALARS],
        out_specs=WHOLE,
        compiler_params=params(),
        name="bounds",
    )(lengths)


def key_places(rows, key_rows, distances):
    tile, split = lax.axis_index("tok"), lax.axis_index("section")
    parts = []
    for d in distances:
        base = (tile - d) * rows + split * key_rows
        parts.append(base + lax.broadcasted_iota(jnp.int32, (1, key_rows), 1))
    return jnp.concatenate(parts, axis=1)


def scores_of(query, keys):
    return lax.dot_general(
        query, keys, (((1,), (1,)), ((), ())), preferred_element_type=jnp.float32
    )


def attend(factor, query, keys, values, visible, peak, total, sums):
    scores = jnp.where(visible, scores_of(query, keys), LOW)
    top = jnp.maximum(peak, jnp.max(scores, axis=1, keepdims=True))
    weights = jnp.exp2((scores - top) * factor).astype(jnp.bfloat16)
    mixed = jnp.dot(weights, values, preferred_element_type=jnp.float32)
    decay = jnp.exp2((peak - top) * factor)
    size = sums.shape[1]
    return top, total * decay + mixed[:, size:], sums * decay + mixed[:, :size]


def gathered(refs, size):
    keys = jnp.concatenate([ref[:, :size] for ref in refs], axis=0)
    values = jnp.concatenate([ref[:, size:] for ref in refs], axis=0)
    ones = jnp.ones((values.shape[0], LANES), values.dtype)
    return keys, jnp.concatenate([values, ones], axis=1)


def stage_kernel(factor, size, key_rows, stage, begin_ref, q_ref, *refs):
    first, last = stage == 0, stage == len(STAGES) - 1
    arrivals = STAGES[stage]
    rows, width = q_ref.shape
    heads = width // size
    begin = begin_ref[:, :1]
    if not first:
        sums_in, totals_in, stats_in, *refs = refs
    if last:
        *kv_refs, out_ref = refs
    else:
        *kv_refs, sums_out, totals_out, stats_out = refs
    if first:
        place = lax.axis_index("tok") * rows + lax.broadcasted_iota(jnp.int32, (rows, 1), 0)
        own_keys, own_values = gathered(kv_refs[:1], size)
        own_place = key_places(rows, key_rows, (0,))
        own_visible = (own_place <= place) & (own_place >= begin)
        arrivals, kv_refs = arrivals[1:], kv_refs[1:]
    keys, values = gathered(kv_refs, size)
    distances = [d for arrival in arrivals for d in distances_of(arrival)]
    visible = key_places(rows, key_rows, distances) >= begin
    lane = lax.broadcasted_iota(jnp.int32, (rows, LANES), 1)
    stats = jnp.full((rows, LANES), LOW, jnp.float32)
    packed = jnp.ones((rows, LANES), jnp.float32)
    for h in range(heads):
        cols = slice(h * size, (h + 1) * size)
        query = q_ref[:, cols]
        if first:
            state = (
                jnp.full((rows, 1), FLOOR, jnp.float32),
                jnp.zeros((rows, LANES), jnp.float32),
                jnp.zeros((rows, size), jnp.float32),
            )
            state = attend(factor, query, own_keys, own_values, own_visible, *state)
        else:
            state = (stats_in[:, h : h + 1], totals_in[:, cols], sums_in[:, cols])
        peak, total, sums = attend(factor, query, keys, values, visible, *state)
        if not last:
            stats = jnp.where(lane == h, peak, stats)
            totals_out[:, cols] = total
            sums_out[:, cols] = sums
            continue
        stats = jnp.where(lane == h, peak, stats)
        packed = jnp.where(lane == h, total, packed)
        out_ref[:rows, cols] = (sums / jnp.maximum(total, 1e-30)).astype(jnp.bfloat16)
    if not last:
        stats_out[...] = stats
        return
    stats = stats * factor + jnp.log2(jnp.maximum(packed, 1e-30))
    stats = jnp.where(packed > 0.0, stats, LOW)
    levels = jnp.transpose(stats)[:8]
    high = levels.astype(jnp.bfloat16).astype(jnp.float32)
    rest = levels - high
    middle = rest.astype(jnp.bfloat16).astype(jnp.float32)
    low = rest - middle
    row = lax.broadcasted_iota(jnp.int32, high.shape, 0)
    packed = jnp.concatenate([jnp.where(row < 4, high, pltpu.roll(middle, 4, 0)), low], axis=0)
    spare = jnp.zeros((STAT_ROWS, width - rows), jnp.float32)
    out_ref[rows:, :] = jnp.concatenate([packed, spare], axis=1).astype(jnp.bfloat16)


def merge_kernel(size, *refs):
    *parts, out_ref = refs
    rows = out_ref.shape[0]
    heads = out_ref.shape[1] // size
    levels = []
    for part in parts:
        packed = part[rows:, :].astype(jnp.float32)[:, :rows]
        levels.append((packed[:8] + pltpu.roll(packed[:8], 4, 0)) + packed[8:])
    top = functools.reduce(jnp.maximum, levels)
    terms = [jnp.exp2(level - top) for level in levels]
    total = (terms[0] + terms[2]) + (terms[1] + terms[3])
    shares = [term / total for term in terms]
    blank = jnp.zeros((LANES - 8 * len(parts), rows), jnp.float32)
    shares = jnp.transpose(jnp.concatenate(shares + [blank], axis=0))
    for h in range(heads):
        cols = slice(h * size, (h + 1) * size)
        terms = [
            part[:rows, cols].astype(jnp.float32) * shares[:, 8 * i + h : 8 * i + h + 1]
            for i, part in enumerate(parts)
        ]
        out_ref[:, cols] = ((terms[0] + terms[2]) + (terms[1] + terms[3])).astype(jnp.bfloat16)


def params():
    return pltpu.CompilerParams(vmem_limit_bytes=40 * 1024 * 1024)


def cost(rows, heads, keys, size):
    pairs = rows * heads * keys
    return pl.CostEstimate(
        flops=4 * pairs * size, bytes_accessed=2 * rows * heads * size, transcendentals=pairs
    )


def stage_call(factor, size, key_rows, stage, begin, queries, state, chunks):
    rows, width = queries.shape
    keys = sum(len(distances_of(arrival)) for arrival in STAGES[stage]) * key_rows
    if stage == len(STAGES) - 1:
        out_shape = jax.ShapeDtypeStruct((rows + STAT_ROWS, width), jnp.bfloat16)
        out_specs = WHOLE
    else:
        out_shape = (
            jax.ShapeDtypeStruct((rows, width), jnp.float32),
            jax.ShapeDtypeStruct((rows, width), jnp.float32),
            jax.ShapeDtypeStruct((rows, LANES), jnp.float32),
        )
        out_specs = (WHOLE, WHOLE, WHOLE)
    return pl.pallas_call(
        functools.partial(stage_kernel, factor, size, key_rows, stage),
        out_shape=out_shape,
        in_specs=[WHOLE] * (2 + len(state) + len(chunks)),
        out_specs=out_specs,
        compiler_params=params(),
        cost_estimate=cost(rows, width // size, keys, size),
        name="attend" + str(stage),
    )(begin, queries, *state, *chunks)


def merge_call(size, rows, parts):
    width = parts[0].shape[1]
    return pl.pallas_call(
        functools.partial(merge_kernel, size),
        out_shape=jax.ShapeDtypeStruct((rows, width), jnp.bfloat16),
        in_specs=[WHOLE] * len(parts),
        out_specs=WHOLE,
        compiler_params=params(),
        name="merge",
    )(*parts)


def shards(tiles, splits, queries, key_values, lengths):
    rows = queries.shape[0]
    key_rows = key_values.shape[2]
    size = key_values.shape[4] // 2
    factor = size ** (-0.5) * math.log2(math.e)
    own = key_values.reshape(key_rows, 2 * size)
    held = {0: (own, 0)}
    arrived = []
    begin = bounds_call(lengths, rows)
    for index, (by, carried) in enumerate(PLAN):
        cargo = joined([held[d] for d in carried], key_rows)
        if index == AHEAD:
            chunks = [own, *(arrived[arrival] for arrival in STAGES[0][1:])]
            state = stage_call(factor, size, key_rows, 0, begin, queries, (), chunks)
            cargo, state = lax.optimization_barrier((cargo, state))
        result = shift(cargo, "tok", by, tiles)
        arrived.append(result)
        for i, d in enumerate(carried):
            held[d] = (cargo, i * key_rows)
            held[d + by] = (result, i * key_rows)
    for stage, arrivals in tuple(enumerate(STAGES))[1:]:
        chunks = [arrived[arrival] for arrival in arrivals]
        state = stage_call(factor, size, key_rows, stage, begin, queries, state, chunks)
    part = state
    parts = [part] + [shift(part, "section", by, splits) for by in reversed(range(1, splits))]
    return merge_call(size, rows, parts)


def solution(mesh):
    return jax.shard_map(
        functools.partial(shards, mesh.shape["tok"], mesh.shape["section"]),
        mesh=mesh,
        in_specs=(P("tok", "head"), P("tok", "section", None, "head", None), P()),
        out_specs=P("tok", "head"),
        check_vma=False,
    )
```

```python
import functools
import math

import jax
import jax.numpy as jnp
from jax import lax
from jax.experimental import pallas as pl
from jax.experimental.pallas import tpu as pltpu
from jax.sharding import PartitionSpec as P

LOW = -1e30
FLOOR = -5e29
LANES = 128
NDOCS = 8
STAT_ROWS = 16
WHOLE = pl.BlockSpec(memory_space=pltpu.VMEM)
SCALARS = pl.BlockSpec(memory_space=pltpu.SMEM)
PLAN = (
    (6, (0,)),
    (6, (6,)),
    (3, (0, 6, 12)),
    (1, (0, 6, 12, 3, 9, 15)),
    (-1, (6, 12, 3, 9, 15)),
)
STAGES = ((-1, 0, 1), (2, 3), (4,))
AHEAD = 3


def distances_of(arrival):
    by, carried = PLAN[arrival]
    return (0,) if arrival < 0 else tuple(d + by for d in carried)


def shift(value, axis, by, count):
    return lax.ppermute(value, axis, [(i, (i + by) % count) for i in range(count)])


def joined(pieces, key_rows):
    runs = []
    for array, row in pieces:
        if runs and runs[-1][0] is array and runs[-1][2] == row:
            runs[-1][2] = row + key_rows
        else:
            runs.append([array, row, row + key_rows])
    cuts = [array if hi - lo == array.shape[0] else array[lo:hi] for array, lo, hi in runs]
    return jnp.concatenate(cuts) if len(cuts) > 1 else cuts[0]


def query_bounds(lengths, rows):
    place = lax.axis_index("tok") * rows + lax.broadcasted_iota(jnp.int32, (rows, LANES), 0)
    begin = jnp.zeros((rows, LANES), jnp.int32)
    end = jnp.int32(0)
    for i in range(NDOCS):
        end = end + lengths[i]
        begin = jnp.where(end <= place, end, begin)
    return begin


def bounds_kernel(lengths, begin_ref):
    begin_ref[...] = query_bounds(lengths, begin_ref.shape[0])


def bounds_call(lengths, rows):
    return pl.pallas_call(
        bounds_kernel,
        out_shape=jax.ShapeDtypeStruct((rows, LANES), jnp.int32),
        in_specs=[SCALARS],
        out_specs=WHOLE,
        compiler_params=params(),
        name="bounds",
    )(lengths)


def key_places(rows, key_rows, distances):
    tile, split = lax.axis_index("tok"), lax.axis_index("section")
    parts = []
    for d in distances:
        base = (tile - d) * rows + split * key_rows
        parts.append(base + lax.broadcasted_iota(jnp.int32, (1, key_rows), 1))
    return jnp.concatenate(parts, axis=1)


def scores_of(query, keys):
    return lax.dot_general(
        query, keys, (((1,), (1,)), ((), ())), preferred_element_type=jnp.float32
    )


def attend(factor, query, keys, values, visible, peak, total, sums):
    scores = jnp.where(visible, scores_of(query, keys), LOW)
    top = jnp.maximum(peak, jnp.max(scores, axis=1, keepdims=True))
    weights = jnp.exp2((scores - top) * factor).astype(jnp.bfloat16)
    mixed = jnp.dot(weights, values, preferred_element_type=jnp.float32)
    decay = jnp.exp2((peak - top) * factor)
    size = sums.shape[1]
    return top, total * decay + mixed[:, size:], sums * decay + mixed[:, :size]


def gathered(refs, size):
    keys = jnp.concatenate([ref[:, :size] for ref in refs], axis=0)
    values = jnp.concatenate([ref[:, size:] for ref in refs], axis=0)
    ones = jnp.ones((values.shape[0], LANES), values.dtype)
    return keys, jnp.concatenate([values, ones], axis=1)


def stage_kernel(factor, size, key_rows, stage, begin_ref, q_ref, *refs):
    first, last = stage == 0, stage == len(STAGES) - 1
    arrivals = STAGES[stage]
    rows, width = q_ref.shape
    heads = width // size
    begin = begin_ref[:, :1]
    if not first:
        sums_in, totals_in, stats_in, *refs = refs
    if last:
        *kv_refs, out_ref = refs
    else:
        *kv_refs, sums_out, totals_out, stats_out = refs
    if first:
        place = lax.axis_index("tok") * rows + lax.broadcasted_iota(jnp.int32, (rows, 1), 0)
        own_keys, own_values = gathered(kv_refs[:1], size)
        own_place = key_places(rows, key_rows, (0,))
        own_visible = (own_place <= place) & (own_place >= begin)
        arrivals, kv_refs = arrivals[1:], kv_refs[1:]
    keys, values = gathered(kv_refs, size)
    distances = [d for arrival in arrivals for d in distances_of(arrival)]
    visible = key_places(rows, key_rows, distances) >= begin
    lane = lax.broadcasted_iota(jnp.int32, (rows, LANES), 1)
    stats = jnp.full((rows, LANES), LOW, jnp.float32)
    packed = jnp.ones((rows, LANES), jnp.float32)
    for h in range(heads):
        cols = slice(h * size, (h + 1) * size)
        query = q_ref[:, cols]
        if first:
            state = (
                jnp.full((rows, 1), FLOOR, jnp.float32),
                jnp.zeros((rows, LANES), jnp.float32),
                jnp.zeros((rows, size), jnp.float32),
            )
            state = attend(factor, query, own_keys, own_values, own_visible, *state)
        else:
            state = (stats_in[:, h : h + 1], totals_in[:, cols], sums_in[:, cols])
        peak, total, sums = attend(factor, query, keys, values, visible, *state)
        if not last:
            stats = jnp.where(lane == h, peak, stats)
            totals_out[:, cols] = total
            sums_out[:, cols] = sums
            continue
        stats = jnp.where(lane == h, peak, stats)
        packed = jnp.where(lane == h, total, packed)
        out_ref[:rows, cols] = (sums / jnp.maximum(total, 1e-30)).astype(jnp.bfloat16)
    if not last:
        stats_out[...] = stats
        return
    stats = stats * factor + jnp.log2(jnp.maximum(packed, 1e-30))
    stats = jnp.where(packed > 0.0, stats, LOW)
    levels = jnp.transpose(stats)[:8]
    high = levels.astype(jnp.bfloat16).astype(jnp.float32)
    rest = levels - high
    middle = rest.astype(jnp.bfloat16).astype(jnp.float32)
    low = rest - middle
    row = lax.broadcasted_iota(jnp.int32, high.shape, 0)
    packed = jnp.concatenate([jnp.where(row < 4, high, pltpu.roll(middle, 4, 0)), low], axis=0)
    spare = jnp.zeros((STAT_ROWS, width - rows), jnp.float32)
    out_ref[rows:, :] = jnp.concatenate([packed, spare], axis=1).astype(jnp.bfloat16)


def merge_kernel(size, *refs):
    *parts, out_ref = refs
    rows = out_ref.shape[0]
    heads = out_ref.shape[1] // size
    levels = []
    for part in parts:
        packed = part[rows:, :].astype(jnp.float32)[:, :rows]
        levels.append((packed[:8] + pltpu.roll(packed[:8], 4, 0)) + packed[8:])
    top = functools.reduce(jnp.maximum, levels)
    terms = [jnp.exp2(level - top) for level in levels]
    total = (terms[0] + terms[1]) + (terms[2] + terms[3])
    shares = [term / total for term in terms]
    blank = jnp.zeros((LANES - 8 * len(parts), rows), jnp.float32)
    shares = jnp.transpose(jnp.concatenate(shares + [blank], axis=0))
    for h in range(heads):
        cols = slice(h * size, (h + 1) * size)
        terms = [
            part[:rows, cols].astype(jnp.float32) * shares[:, 8 * i + h : 8 * i + h + 1]
            for i, part in enumerate(parts)
        ]
        out_ref[:, cols] = ((terms[0] + terms[1]) + (terms[2] + terms[3])).astype(jnp.bfloat16)


def params():
    return pltpu.CompilerParams(vmem_limit_bytes=40 * 1024 * 1024)


def cost(rows, heads, keys, size):
    pairs = rows * heads * keys
    return pl.CostEstimate(
        flops=4 * pairs * size, bytes_accessed=2 * rows * heads * size, transcendentals=pairs
    )


def stage_call(factor, size, key_rows, stage, begin, queries, state, chunks):
    rows, width = queries.shape
    keys = sum(len(distances_of(arrival)) for arrival in STAGES[stage]) * key_rows
    if stage == len(STAGES) - 1:
        out_shape = jax.ShapeDtypeStruct((rows + STAT_ROWS, width), jnp.bfloat16)
        out_specs = WHOLE
    else:
        out_shape = (
            jax.ShapeDtypeStruct((rows, width), jnp.float32),
            jax.ShapeDtypeStruct((rows, width), jnp.float32),
            jax.ShapeDtypeStruct((rows, LANES), jnp.float32),
        )
        out_specs = (WHOLE, WHOLE, WHOLE)
    return pl.pallas_call(
        functools.partial(stage_kernel, factor, size, key_rows, stage),
        out_shape=out_shape,
        in_specs=[WHOLE] * (2 + len(state) + len(chunks)),
        out_specs=out_specs,
        compiler_params=params(),
        cost_estimate=cost(rows, width // size, keys, size),
        name="attend" + str(stage),
    )(begin, queries, *state, *chunks)


def merge_call(size, rows, parts):
    width = parts[0].shape[1]
    return pl.pallas_call(
        functools.partial(merge_kernel, size),
        out_shape=jax.ShapeDtypeStruct((rows, width), jnp.bfloat16),
        in_specs=[WHOLE] * len(parts),
        out_specs=WHOLE,
        compiler_params=params(),
        name="merge",
    )(*parts)


def shards(tiles, splits, queries, key_values, lengths):
    rows = queries.shape[0]
    key_rows = key_values.shape[2]
    size = key_values.shape[4] // 2
    factor = size ** (-0.5) * math.log2(math.e)
    own = key_values.reshape(key_rows, 2 * size)
    held = {0: (own, 0)}
    arrived = []
    begin = bounds_call(lengths, rows)
    for index, (by, carried) in enumerate(PLAN):
        cargo = joined([held[d] for d in carried], key_rows)
        if index == AHEAD:
            chunks = [own, *(arrived[arrival] for arrival in STAGES[0][1:])]
            state = stage_call(factor, size, key_rows, 0, begin, queries, (), chunks)
            cargo, state = lax.optimization_barrier((cargo, state))
        result = shift(cargo, "tok", by, tiles)
        arrived.append(result)
        for i, d in enumerate(carried):
            held[d] = (cargo, i * key_rows)
            held[d + by] = (result, i * key_rows)
    for stage, arrivals in tuple(enumerate(STAGES))[1:]:
        chunks = [arrived[arrival] for arrival in arrivals]
        state = stage_call(factor, size, key_rows, stage, begin, queries, state, chunks)
    part = state
    parts = [part] + [shift(part, "section", by, splits) for by in (2, 3, 1)]
    return merge_call(size, rows, parts)


def solution(mesh):
    return jax.shard_map(
        functools.partial(shards, mesh.shape["tok"], mesh.shape["section"]),
        mesh=mesh,
        in_specs=(P("tok", "head"), P("tok", "section", None, "head", None), P()),
        out_specs=P("tok", "head"),
        check_vma=False,
    )
```
